32 devices in a mesh: ia: 2 (over y), ib: 4 (over z), op: 4 (over x, core).
Axes of the slice: x: 2, y: 2, z: 4, core: 2. Of those that a mesh axis runs over, the one named last changes fastest.
Arguments:
- fit_coefficients: bfloat16 [2, 3072, 4096], P('ia', ('ib', 'op')), may hold values from -0.09375 to 0.09375
- three_center: bfloat16 [2, 4096, 3072], P(None, None, ('ib', 'op')), may hold values from -6 to 6
- amplitudes: bfloat16 [32, 3072, 3072], P('op', ('ia', 'ib')), may hold values from -0.001953125 to 0.001953125
- pair_list: int32 [32, 2], P('op'), may hold values from 0 to 255
- slot_tiles: int32 [8], replicated, may hold values from 0 to 7, each once
- energy_occupied: float32 [256], replicated, may hold values from -1.2 to -0.4
- energy_left: float32 [2], P('ia'), may hold values from 0.3 to 2.5
- energy_right: float32 [2], replicated, may hold values from 0.3 to 2.5
Outputs:
- update: float32 [32, 2, 2], P('op', 'ia')
The draws below stay inside these ranges and needn't reach their ends.
Inputs may be any that keep to these rules, and one draw needn't show every extreme that they name: `slot_tiles`: each tile number stands in exactly one slot.
All inputs are finite; a program needn't handle non-finite values.
Results may differ from the reference program's by a relative error of at most 0.0029.
Values may be sent and summed in bfloat16 or wider, within the bound.
A program may use at most 128 MiB of HBM per device.

```python
import jax
import jax.numpy as jnp
from jax import lax

V = 3072
NAUX = 4096
NOCC = 256
PAIRS = 32
NA = 2
NB = 2
NTILE = 8
TW = 384


def place_ends(values, own_key, least, largest):
    extent = values.shape
    place = [jax.random.randint(jax.random.fold_in(own_key, axis), (), 0, extent[axis]) for axis in range(len(extent))]
    values = values.at[tuple(place)].set(least)
    longest = extent.index(max(extent))
    place[longest] = (place[longest] + 1) % extent[longest]
    return values.at[tuple(place)].set(largest)


def levels(rng, shape, shards, low, high):
    level = 1.0
    for dim, parts in shards:
        draws = jax.random.uniform(jax.random.fold_in(jax.random.fold_in(rng, 6), dim), (parts,), jnp.float32, low / len(shards), high / len(shards))
        level = level * jnp.repeat(jnp.exp(draws), shape[dim] // parts).reshape((-1,) + (1,) * (len(shape) - 1 - dim))
    return level


def scatter_about(stream_key, shape, deviation, limit, cuts=(), held_as=jnp.bfloat16):
    factor_of = levels(stream_key, shape, cuts, -0.22, 0.18) if cuts else 1.0
    result = jax.random.normal(stream_key, shape, jnp.float32) * deviation * factor_of
    return jnp.minimum(jnp.maximum(result, -limit), limit).astype(held_as)


def setup_inputs(seed: int = 0) -> dict:
    key_of = jax.random.split(jax.random.key(seed), 9)
    fit_coefficients = scatter_about(key_of[0], (NA, V, NAUX), NAUX ** -0.5, 0.09375, ((0, 2), (1, 16)))
    three_center = scatter_about(key_of[1], (NB, NAUX, V), 1.0, 6.0, ((2, 16),))
    amplitudes = scatter_about(key_of[2], (PAIRS, V, V), (V * V) ** -0.5, 0.001953125, ((0, 4), (1, 8)))
    pair_list = place_ends(jax.random.randint(key_of[3], (PAIRS, 2), 0, NOCC), jax.random.fold_in(key_of[3], 1), 0, NOCC - 1).astype(jnp.int32)
    slot_tiles = jax.random.permutation(key_of[4], NTILE).astype(jnp.int32)
    energy_occupied = jnp.clip(jax.random.uniform(key_of[5], (NOCC,), jnp.float32, -1.2, -0.4), -1.2, -0.4)
    energy_left = jnp.clip(0.3 + 2.2 * jax.random.uniform(key_of[6], (NA,), jnp.float32) ** levels(key_of[6], (NA,), ((0, 2),), -0.2, 0.2), 0.3, 2.5)
    energy_right = jnp.clip(jax.random.uniform(key_of[7], (NB,), jnp.float32, 0.3, 2.5), 0.3, 2.5)
    return dict(fit_coefficients=fit_coefficients, three_center=three_center, amplitudes=amplitudes, pair_list=pair_list, slot_tiles=slot_tiles, energy_occupied=energy_occupied, energy_left=energy_left, energy_right=energy_right)


laplace_points = (0.06, 0.25, 0.7, 1.6, 3.5)
laplace_weights = (0.16, 0.36, 0.62, 1.0, 1.7)


def reference(fit_coefficients, three_center, amplitudes, pair_list, slot_tiles, energy_occupied, energy_left, energy_right):
    flat_amplitudes = amplitudes.reshape(PAIRS, V * V)

    def one_entry(position):
        left_index = position // NB
        right_index = position % NB
        fit_row = lax.dynamic_index_in_dim(fit_coefficients, left_index, 0, keepdims=False)
        center_row = lax.dynamic_index_in_dim(three_center, right_index, 0, keepdims=False)
        integrals = jnp.dot(fit_row, center_row, preferred_element_type=jnp.float32).astype(jnp.bfloat16)
        integrals = integrals.reshape(NTILE, TW, V)[slot_tiles].reshape(V * V)
        return jnp.dot(flat_amplitudes, integrals, preferred_element_type=jnp.float32)

    residual = lax.map(one_entry, jnp.arange(NA * NB, dtype=jnp.int32))
    residual = jnp.transpose(residual).reshape(PAIRS, NA, NB)
    occupied_sum = energy_occupied[pair_list[:, 0]] + energy_occupied[pair_list[:, 1]]
    denominator = energy_left[None, :, None] + energy_right[None, None, :] - occupied_sum[:, None, None]
    factor = jnp.zeros_like(denominator)
    for point, weight in zip(laplace_points, laplace_weights):
        factor = factor + weight * jnp.exp(-point * denominator)
    return residual * factor
```

```python
import functools

import jax
import jax.numpy as jnp
from jax import lax
from jax.experimental import pallas as pl
from jax.experimental.pallas import tpu as pltpu
from jax.sharding import PartitionSpec as P

laplace_points = (0.06, 0.25, 0.7, 1.6, 3.5)
laplace_weights = (0.16, 0.36, 0.62, 1.0, 1.7)
lanes = 128


def tiles_kernel(slots_ref, *refs):
    *coefficient_refs, center_ref, out_ref = refs
    rows = jnp.concatenate([r[0] for r in coefficient_refs], axis=0)
    product = lax.dot_general(
        center_ref[...], rows, (((1,), (1,)), ((), ())), preferred_element_type=jnp.float32
    ).astype(jnp.bfloat16)
    for i in range(len(coefficient_refs)):
        out_ref[i] = product[:, i * lanes : (i + 1) * lanes]


def integral_tiles(coefficients, center, slot_tiles, pair=2):
    slots, width, aux = coefficients.shape
    columns = center.shape[0]
    specs = [
        pl.BlockSpec((1, width, aux), lambda s, t, i=i: (t[s * pair + i], 0, 0)) for i in range(pair)
    ]
    return pl.pallas_call(
        tiles_kernel,
        out_shape=jax.ShapeDtypeStruct((slots, columns, width), jnp.bfloat16),
        grid_spec=pltpu.PrefetchScalarGridSpec(
            num_scalar_prefetch=1,
            grid=(slots // pair,),
            in_specs=[*specs, pl.BlockSpec((columns, aux), lambda s, t: (0, 0))],
            out_specs=pl.BlockSpec((pair, columns, width), lambda s, t: (s, 0, 0)),
        ),
        compiler_params=pltpu.CompilerParams(vmem_limit_bytes=40 * 2**20),
        cost_estimate=pl.CostEstimate(
            flops=2 * slots * columns * width * aux,
            bytes_accessed=2 * (slots * width * aux + columns * aux + slots * columns * width),
            transcendentals=0,
        ),
    )(slot_tiles, *([coefficients] * pair), center)


def contract_kernel(amps_ref, tiles_ref, out_ref, total):
    step = pl.program_id(0) * pl.num_programs(1) + pl.program_id(1)
    steps = pl.num_programs(0) * pl.num_programs(1)
    pairs, halves, rows, depth = amps_ref.shape
    left = amps_ref[...].reshape(pairs * halves * rows, depth)
    _, merged, a_count, _, b_count, share, width = tiles_ref.shape
    right = jnp.concatenate(
        [
            jnp.concatenate([tiles_ref[0, m, a, 0, b] for m in range(merged)], axis=0)
            for a in range(a_count)
            for b in range(b_count)
        ],
        axis=1,
    )
    product = jnp.dot(left, right, preferred_element_type=jnp.float32)

    @pl.when(step == 0)
    def _():
        total[...] = product

    @pl.when(step > 0)
    def _():
        total[...] += product

    @pl.when(step == steps - 1)
    def _():
        count = total.shape[1]
        row = lax.broadcasted_iota(jnp.int32, (halves * rows, count), 0)
        column = lax.broadcasted_iota(jnp.int32, (halves * rows, count), 1) % width
        kept = row == column
        for p in range(pairs):
            block = total[p * halves * rows : (p + 1) * halves * rows, :]
            out_ref[p : p + 1, :] = jnp.sum(jnp.where(kept, block, 0.0), axis=0, keepdims=True)


def contract(amps, tiles, chunk):
    pairs, halves, _, _ = amps.shape
    groups, merged, a_count, ib_count, b_count, share, width = tiles.shape
    rows = width // halves
    depth = merged * share
    columns = a_count * b_count * width
    return pl.pallas_call(
        contract_kernel,
        out_shape=jax.ShapeDtypeStruct((pairs, columns), jnp.float32),
        grid=(ib_count, groups),
        in_specs=[
            pl.BlockSpec((pairs, halves, rows, depth), lambda i, g: (0, 0, chunk, i * groups + g)),
            pl.BlockSpec(
                (1, merged, a_count, 1, b_count, share, width), lambda i, g: (g, 0, 0, i, 0, 0, 0)
            ),
        ],
        out_specs=pl.BlockSpec((pairs, columns), lambda i, g: (0, 0)),
        scratch_shapes=[pltpu.VMEM((pairs * halves * rows, columns), jnp.float32)],
        compiler_params=pltpu.CompilerParams(vmem_limit_bytes=40 * 2**20),
        cost_estimate=pl.CostEstimate(
            flops=2 * pairs * width * columns * depth * ib_count * groups,
            bytes_accessed=2 * (pairs * width * depth * ib_count * groups + tiles.size),
            transcendentals=0,
        ),
    )(amps, tiles)


def chunked(fit_coefficients, three_center, amplitudes, slot_tiles):
    left_rows, own_rows, aux = fit_coefficients.shape
    right_rows, _, share = three_center.shape
    local_pairs, tile_width, full = amplitudes.shape
    left_count, right_count = lax.axis_size("ia"), lax.axis_size("ib")
    group_count = lax.axis_size("op")
    slots = left_count * right_count
    halves = tile_width // own_rows
    rows = lanes // halves
    center = jnp.transpose(three_center, (0, 2, 1)).reshape(right_rows * share, aux)
    amps = amplitudes.reshape(local_pairs, halves, own_rows, full)
    value = 0.0
    for j in range(own_rows // rows):
        piece = lax.all_gather(
            fit_coefficients[0, j * rows : (j + 1) * rows], ("ib", "op"), axis=0, tiled=True
        )
        tiles = integral_tiles(piece.reshape(slots, lanes, aux), center, slot_tiles)
        arrived = lax.all_to_all(tiles, ("ia", "ib"), split_axis=0, concat_axis=0, tiled=True)
        spread = lax.all_gather(arrived, "op", axis=0, tiled=True)
        spread = spread.reshape(
            group_count // 2, 2, left_count, right_count, right_rows, share, lanes
        )
        value = value + contract(amps, spread, j)
    return value.reshape(local_pairs, left_count, right_rows, lanes).sum(axis=3)


def whole_at_once(fit_coefficients, three_center, amplitudes, slot_tiles):
    left_rows = fit_coefficients.shape[0]
    right_rows = three_center.shape[0]
    share = three_center.shape[2]
    tile_width = amplitudes.shape[1]
    local_pairs = amplitudes.shape[0]
    left_count, right_count = lax.axis_size("ia"), lax.axis_size("ib")
    group_count = lax.axis_size("op")
    slot_count = left_count * right_count
    tiles = jnp.einsum(
        "oiu,tup->otip",
        lax.all_gather(fit_coefficients, ("ib", "op"), axis=1, tiled=True),
        three_center,
        preferred_element_type=jnp.float32,
    ).astype(jnp.bfloat16)
    tiles = tiles.reshape(left_rows, right_rows, slot_count, tile_width, share)
    ordered = jnp.concatenate(
        [lax.dynamic_slice_in_dim(tiles, slot_tiles[s], 1, axis=2) for s in range(slot_count)],
        axis=2,
    )
    arrived = lax.all_to_all(ordered, ("ia", "ib"), split_axis=2, concat_axis=0, tiled=True)
    received = arrived.reshape(left_count, right_count, left_rows, right_rows, tile_width, share)
    split_amps = amplitudes.reshape(local_pairs, tile_width, right_count, group_count * share)
    value = jnp.einsum(
        "pkie,aiobke->paob",
        split_amps,
        lax.all_gather(received, "op", axis=5, tiled=True),
        preferred_element_type=jnp.float32,
    )
    return value.reshape(local_pairs, left_count * left_rows, right_rows)


def per_device(
    fit_coefficients,
    three_center,
    amplitudes,
    pair_list,
    slot_tiles,
    energy_occupied,
    energy_left,
    energy_right,
):
    left_rows, own_rows, _ = fit_coefficients.shape
    right_rows, _, share = three_center.shape
    local_pairs, tile_width, _ = amplitudes.shape
    halves = tile_width // own_rows
    fits = (
        left_rows == 1
        and halves > 0
        and tile_width == halves * own_rows
        and lanes % max(halves, 1) == 0
        and own_rows % (lanes // max(halves, 1)) == 0
        and (lanes // max(halves, 1)) % 16 == 0
        and lax.axis_size("op") % 2 == 0
        and (2 * share) % lanes == 0
        and share % 16 == 0
        and (lax.axis_size("ia") * lax.axis_size("ib")) % 2 == 0
    )
    partial_value = (chunked if fits else whole_at_once)(
        fit_coefficients, three_center, amplitudes, slot_tiles
    )
    summed = lax.psum(partial_value, ("ia", "ib"))
    owned = lax.dynamic_slice(
        summed,
        (0, lax.axis_index("ia") * left_rows, 0),
        (local_pairs, left_rows, right_rows),
    )
    occupied = energy_occupied.shape[0]
    column = lax.broadcasted_iota(jnp.int32, (local_pairs, occupied), 1)
    occupied_one = jnp.sum(
        jnp.where(pair_list[:, 0:1] == column, energy_occupied[None, :], 0.0), axis=1
    )
    occupied_two = jnp.sum(
        jnp.where(pair_list[:, 1:2] == column, energy_occupied[None, :], 0.0), axis=1
    )
    occupied_sum = occupied_one + occupied_two
    denominator = (
        energy_left[None, :, None] + energy_right[None, None, :] - occupied_sum[:, None, None]
    )
    factor = jnp.zeros_like(denominator)
    for point, weight in zip(laplace_points, laplace_weights):
        factor = factor + weight * jnp.exp(-point * denominator)
    return owned * factor


def solution(mesh):
    placed = (
        P("ia", ("ib", "op"), None),
        P(None, None, ("ib", "op")),
        P("op", ("ia", "ib"), None),
        P("op", None),
        P(),
        P(),
        P("ia"),
        P(),
    )
    return jax.shard_map(
        per_device, mesh=mesh, in_specs=placed, out_specs=P("op", "ia", None), check_vma=False
    )
```

```python
import functools

import jax
import jax.numpy as jnp
from jax import lax
from jax.experimental import pallas as pl
from jax.experimental.pallas import tpu as pltpu
from jax.sharding import PartitionSpec as P

laplace_points = (0.06, 0.25, 0.7, 1.6, 3.5)
laplace_weights = (0.16, 0.36, 0.62, 1.0, 1.7)
lanes = 128


def tiles_kernel(slots_ref, coefficient_ref, center_ref, out_ref):
    out_ref[0] = lax.dot_general(
        center_ref[...],
        coefficient_ref[0],
        (((1,), (1,)), ((), ())),
        preferred_element_type=jnp.float32,
    ).astype(jnp.bfloat16)


def integral_tiles(coefficients, center, slot_tiles):
    slots, width, aux = coefficients.shape
    columns = center.shape[0]
    return pl.pallas_call(
        tiles_kernel,
        out_shape=jax.ShapeDtypeStruct((slots, columns, width), jnp.bfloat16),
        grid_spec=pltpu.PrefetchScalarGridSpec(
            num_scalar_prefetch=1,
            grid=(slots,),
            in_specs=[
                pl.BlockSpec((1, width, aux), lambda s, t: (t[s], 0, 0)),
                pl.BlockSpec((columns, aux), lambda s, t: (0, 0)),
            ],
            out_specs=pl.BlockSpec((1, columns, width), lambda s, t: (s, 0, 0)),
        ),
        compiler_params=pltpu.CompilerParams(vmem_limit_bytes=56 * 2**20),
        cost_estimate=pl.CostEstimate(
            flops=2 * slots * columns * width * aux,
            bytes_accessed=2 * (slots * width * aux + columns * aux + slots * columns * width),
            transcendentals=0,
        ),
    )(slot_tiles, coefficients, center)


def spread_kernel(
    left_count, right_count, right_rows, tiles_ref, amps_hbm, out_ref, amps_ref, held, total, part, sums,
    amps_sem, own_sem, send_slot, recv_slot, send_far, recv_far, send_near, recv_near, send_sum, recv_sum,
):
    slots = left_count * right_count
    ia, ib, op = lax.axis_index("ia"), lax.axis_index("ib"), lax.axis_index("op")
    me = ia * right_count + ib
    near = (op // 2) * 2 + 1 - op % 2
    far = (op + 2) % 4
    diagonal = (near + 2) % 4
    pairs, width, _ = amps_ref.shape
    share = tiles_ref.shape[1] // right_rows
    depth = 4 * share
    parts = width // lanes
    columns = slots // right_count * right_rows * lanes
    mesh_ids = pl.DeviceIdType.MESH

    def slot_device(s):
        return (s // right_count, s % right_count, op)

    near_device, far_device = (ia, ib, near), (ia, ib, far)

    load = pltpu.make_async_copy(amps_hbm, amps_ref, amps_sem)
    load.start()
    own = pltpu.make_async_copy(tiles_ref.at[me], held.at[op, me], own_sem)
    own.start()

    barrier = pltpu.get_barrier_semaphore()
    for k in range(1, slots):
        pl.semaphore_signal(
            barrier, inc=1, device_id=slot_device((me + k) % slots), device_id_type=mesh_ids
        )
    for device in (near_device, far_device):
        pl.semaphore_signal(barrier, inc=1, device_id=device, device_id_type=mesh_ids)
    pl.semaphore_wait(barrier, slots + 1)

    def to_slot(k):
        target = (me + k) % slots
        return pltpu.make_async_remote_copy(
            src_ref=tiles_ref.at[target], dst_ref=held.at[op, me],
            send_sem=send_slot.at[k], recv_sem=recv_slot.at[k],
            device_id=slot_device(target), device_id_type=mesh_ids,
        )

    def from_slot(k):
        source = (me + slots - k) % slots
        return pltpu.make_async_remote_copy(
            src_ref=tiles_ref.at[source], dst_ref=held.at[op, source],
            send_sem=send_slot.at[k], recv_sem=recv_slot.at[k],
            device_id=slot_device(source), device_id_type=mesh_ids,
        )

    def across(k, row, sends, receives, at, device):
        source = (me + slots - k) % slots
        return pltpu.make_async_remote_copy(
            src_ref=held.at[row, source], dst_ref=held.at[row, source],
            send_sem=sends.at[at], recv_sem=receives.at[at],
            device_id=device, device_id_type=mesh_ids,
        )

    for o in range(right_count):
        for a in range(left_count):
            if o + a > 0:
                to_slot(o + a * right_count).start()
    total[...] = jnp.zeros_like(total)
    own.wait()

    def contract(o):
        for a in range(left_count):
            k = o + a * right_count
            across(k, near, send_near, recv_near, k, near_device).wait_recv()
            across(k, diagonal, send_near, recv_near, slots + k, near_device).wait_recv()
        block = (ib + right_count - o) % right_count

        def one(j, carry):
            across_c = pl.ds(pl.multiple_of(j * lanes, lanes), lanes)
            left = amps_ref[
                :, across_c, pl.ds(pl.multiple_of(block * depth, lanes), depth)
            ].reshape(pairs * lanes, depth)
            right = jnp.concatenate(
                [
                    jnp.concatenate(
                        [
                            held[g, a * right_count + block, b * share : (b + 1) * share, across_c]
                            for g in range(4)
                        ],
                        axis=0,
                    )
                    for a in range(left_count)
                    for b in range(right_rows)
                ],
                axis=1,
            )
            total[...] += jnp.dot(left, right, preferred_element_type=jnp.float32)
            return carry

        lax.fori_loop(0, parts, one, 0)

    def step(o, carry):
        @pl.when(o < right_count)
        def _():
            for a in range(left_count):
                k = o + a * right_count

                @pl.when(k > 0)
                def _():
                    from_slot(k).wait_recv()

                across(k, op, send_far, recv_far, k, far_device).start()
                across(k, op, send_near, recv_near, k, near_device).start()
            for a in range(left_count):
                k = o + a * right_count
                across(k, far, send_far, recv_far, k, far_device).wait_recv()
                across(k, far, send_near, recv_near, slots + k, near_device).start()

        @pl.when(o == 0)
        def _():
            load.wait()

        @pl.when(o > 0)
        def _():
            contract(o - 1)

        return carry

    lax.fori_loop(0, right_count + 1, step, 0)

    row = lax.broadcasted_iota(jnp.int32, (lanes, columns), 0)
    column = lax.broadcasted_iota(jnp.int32, (lanes, columns), 1) % lanes
    for p in range(pairs):
        block = total[p * lanes : (p + 1) * lanes, :]
        part[p : p + 1, :] = jnp.sum(jnp.where(row == column, block, 0.0), axis=0, keepdims=True)

    def to_sum(k):
        return pltpu.make_async_remote_copy(
            src_ref=part, dst_ref=sums.at[k],
            send_sem=send_sum.at[k], recv_sem=recv_sum.at[k],
            device_id=slot_device((me + k) % slots), device_id_type=mesh_ids,
        )

    for k in range(1, slots):
        to_sum(k).start()
    for k in range(slots):
        if k > 0:
            to_slot(k).wait_send()
        across(k, op, send_far, recv_far, k, far_device).wait_send()
        across(k, op, send_near, recv_near, k, near_device).wait_send()
        across(k, far, send_near, recv_near, slots + k, near_device).wait_send()
    value = part[...]
    for k in range(1, slots):
        to_sum(k).wait_recv()
        value = value + sums[k]
    for k in range(1, slots):
        to_sum(k).wait_send()
    out_ref[...] = value


def spread_and_contract(tiles, amplitudes, right_rows):
    slots, rows, width = tiles.shape
    pairs, _, full = amplitudes.shape
    left_count, right_count = lax.axis_size("ia"), lax.axis_size("ib")
    columns = left_count * right_rows * lanes
    dma = pltpu.SemaphoreType.DMA
    return pl.pallas_call(
        functools.partial(spread_kernel, left_count, right_count, right_rows),
        out_shape=jax.ShapeDtypeStruct((pairs, columns), jnp.float32),
        in_specs=[pl.BlockSpec(memory_space=pltpu.VMEM), pl.BlockSpec(memory_space=pl.ANY)],
        out_specs=pl.BlockSpec(memory_space=pltpu.VMEM),
        scratch_shapes=[
            pltpu.VMEM((pairs, width, full), jnp.bfloat16),
            pltpu.VMEM((4, slots, rows, width), jnp.bfloat16),
            pltpu.VMEM((pairs * lanes, columns), jnp.float32),
            pltpu.VMEM((pairs, columns), jnp.float32),
            pltpu.VMEM((slots, pairs, columns), jnp.float32),
            dma, dma,
            dma((slots,)), dma((slots,)), dma((slots,)), dma((slots,)),
            dma((2 * slots,)), dma((2 * slots,)), dma((slots,)), dma((slots,)),
        ],
        compiler_params=pltpu.CompilerParams(
            collective_id=0, has_side_effects=True, vmem_limit_bytes=56 * 2**20
        ),
        cost_estimate=pl.CostEstimate(
            flops=2 * pairs * lanes * columns * full * (width // lanes),
            bytes_accessed=2 * (pairs * width * full + tiles.size),
            transcendentals=0,
        ),
    )(tiles, amplitudes)


def fused(fit_coefficients, three_center, amplitudes, slot_tiles):
    _, own_rows, aux = fit_coefficients.shape
    right_rows, _, share = three_center.shape
    local_pairs, tile_width, _ = amplitudes.shape
    slots = lax.axis_size("ia") * lax.axis_size("ib")
    center = jnp.transpose(three_center, (0, 2, 1)).reshape(right_rows * share, aux)
    gathered = lax.all_gather(fit_coefficients[0], ("ib", "op"), axis=0, tiled=True)
    tiles = integral_tiles(gathered.reshape(slots, tile_width, aux), center, slot_tiles)
    value = spread_and_contract(tiles, amplitudes, right_rows)
    return value.reshape(local_pairs, lax.axis_size("ia"), right_rows, lanes).sum(axis=3)


def whole_at_once(fit_coefficients, three_center, amplitudes, slot_tiles):
    left_rows = fit_coefficients.shape[0]
    right_rows = three_center.shape[0]
    share = three_center.shape[2]
    tile_width = amplitudes.shape[1]
    local_pairs = amplitudes.shape[0]
    left_count, right_count = lax.axis_size("ia"), lax.axis_size("ib")
    group_count = lax.axis_size("op")
    slot_count = left_count * right_count
    tiles = jnp.einsum(
        "oiu,tup->otip",
        lax.all_gather(fit_coefficients, ("ib", "op"), axis=1, tiled=True),
        three_center,
        preferred_element_type=jnp.float32,
    ).astype(jnp.bfloat16)
    tiles = tiles.reshape(left_rows, right_rows, slot_count, tile_width, share)
    ordered = jnp.concatenate(
        [lax.dynamic_slice_in_dim(tiles, slot_tiles[s], 1, axis=2) for s in range(slot_count)],
        axis=2,
    )
    arrived = lax.all_to_all(ordered, ("ia", "ib"), split_axis=2, concat_axis=0, tiled=True)
    received = arrived.reshape(left_count, right_count, left_rows, right_rows, tile_width, share)
    split_amps = amplitudes.reshape(local_pairs, tile_width, right_count, group_count * share)
    value = jnp.einsum(
        "pkie,aiobke->paob",
        split_amps,
        lax.all_gather(received, "op", axis=5, tiled=True),
        preferred_element_type=jnp.float32,
    )
    return value.reshape(local_pairs, left_count * left_rows, right_rows)


def per_device(
    fit_coefficients,
    three_center,
    amplitudes,
    pair_list,
    slot_tiles,
    energy_occupied,
    energy_left,
    energy_right,
):
    left_rows, own_rows, _ = fit_coefficients.shape
    right_rows, _, share = three_center.shape
    local_pairs, tile_width, _ = amplitudes.shape
    arguments = (fit_coefficients, three_center, amplitudes, slot_tiles)
    fits = (
        left_rows == 1
        and lax.axis_size("op") == 4
        and tile_width % lanes == 0
        and (4 * share) % lanes == 0
        and share % 16 == 0
        and local_pairs % 8 == 0
    )
    if fits:
        summed = fused(*arguments)
    else:
        summed = lax.psum(whole_at_once(*arguments), ("ia", "ib"))
    owned = lax.dynamic_slice(
        summed,
        (0, lax.axis_index("ia") * left_rows, 0),
        (local_pairs, left_rows, right_rows),
    )
    occupied = energy_occupied.shape[0]
    column = lax.broadcasted_iota(jnp.int32, (local_pairs, occupied), 1)
    occupied_one = jnp.sum(
        jnp.where(pair_list[:, 0:1] == column, energy_occupied[None, :], 0.0), axis=1
    )
    occupied_two = jnp.sum(
        jnp.where(pair_list[:, 1:2] == column, energy_occupied[None, :], 0.0), axis=1
    )
    occupied_sum = occupied_one + occupied_two
    denominator = (
        energy_left[None, :, None] + energy_right[None, None, :] - occupied_sum[:, None, None]
    )
    factor = jnp.zeros_like(denominator)
    for point, weight in zip(laplace_points, laplace_weights):
        factor = factor + weight * jnp.exp(-point * denominator)
    return owned * factor


def solution(mesh):
    placed = (
        P("ia", ("ib", "op"), None),
        P(None, None, ("ib", "op")),
        P("op", ("ia", "ib"), None),
        P("op", None),
        P(),
        P(),
        P("ia"),
        P(),
    )
    return jax.shard_map(
        per_device, mesh=mesh, in_specs=placed, out_specs=P("op", "ia", None), check_vma=False
    )
```

```python
import functools

import jax
import jax.numpy as jnp
from jax import lax
from jax.experimental import pallas as pl
from jax.experimental.pallas import tpu as pltpu
from jax.sharding import PartitionSpec as P

laplace_points = (0.06, 0.25, 0.7, 1.6, 3.5)
laplace_weights = (0.16, 0.36, 0.62, 1.0, 1.7)
lanes = 128


def tiles_kernel(slots_ref, first_ref, second_ref, center_ref, out_ref):
    rows = jnp.concatenate([first_ref[0], second_ref[0]], axis=0)
    width = first_ref.shape[1]
    product = lax.dot_general(
        center_ref[...], rows, (((1,), (1,)), ((), ())), preferred_element_type=jnp.float32
    ).astype(jnp.bfloat16)
    out_ref[0] = product[:, :width]
    out_ref[1] = product[:, width:]


def integral_tiles(coefficients, center, slot_tiles):
    slots, width, aux = coefficients.shape
    columns = center.shape[0]
    return pl.pallas_call(
        tiles_kernel,
        out_shape=jax.ShapeDtypeStruct((slots, columns, width), jnp.bfloat16),
        grid_spec=pltpu.PrefetchScalarGridSpec(
            num_scalar_prefetch=1,
            grid=(slots // 2,),
            in_specs=[
                pl.BlockSpec((1, width, aux), lambda s, t: (t[2 * s], 0, 0)),
                pl.BlockSpec((1, width, aux), lambda s, t: (t[2 * s + 1], 0, 0)),
                pl.BlockSpec((columns, aux), lambda s, t: (0, 0)),
            ],
            out_specs=pl.BlockSpec((2, columns, width), lambda s, t: (s, 0, 0)),
        ),
        compiler_params=pltpu.CompilerParams(vmem_limit_bytes=56 * 2**20),
        cost_estimate=pl.CostEstimate(
            flops=2 * slots * columns * width * aux,
            bytes_accessed=2 * (slots * width * aux + columns * aux + slots * columns * width),
            transcendentals=0,
        ),
    )(slot_tiles, coefficients, coefficients, center)


def spread_kernel(
    left_count, right_count, right_rows, tiles_ref, amps_hbm, out_ref, amps_ref, held, total, part, sums,
    amps_sem, own_sem, send_slot, recv_slot, send_far, recv_far, send_near, recv_near, send_sum, recv_sum,
):
    slots = left_count * right_count
    ia, ib, op = lax.axis_index("ia"), lax.axis_index("ib"), lax.axis_index("op")
    me = ia * right_count + ib
    near = (op // 2) * 2 + 1 - op % 2
    far = (op + 2) % 4
    diagonal = (near + 2) % 4
    pairs, width, _ = amps_ref.shape
    share = tiles_ref.shape[1] // right_rows
    depth = 4 * share
    parts = width // lanes
    columns = slots // right_count * right_rows * lanes
    mesh_ids = pl.DeviceIdType.MESH

    def slot_device(s):
        return (s // right_count, s % right_count, op)

    near_device, far_device = (ia, ib, near), (ia, ib, far)

    load = pltpu.make_async_copy(amps_hbm, amps_ref, amps_sem)
    load.start()
    own = pltpu.make_async_copy(tiles_ref.at[me], held.at[op, me], own_sem)
    own.start()

    barrier = pltpu.get_barrier_semaphore()
    for k in range(1, slots):
        pl.semaphore_signal(
            barrier, inc=1, device_id=slot_device((me + k) % slots), device_id_type=mesh_ids
        )
    for device in (near_device, far_device):
        pl.semaphore_signal(barrier, inc=1, device_id=device, device_id_type=mesh_ids)
    pl.semaphore_wait(barrier, slots + 1)

    def to_slot(k):
        target = (me + k) % slots
        return pltpu.make_async_remote_copy(
            src_ref=tiles_ref.at[target], dst_ref=held.at[op, me],
            send_sem=send_slot.at[k], recv_sem=recv_slot.at[k],
            device_id=slot_device(target), device_id_type=mesh_ids,
        )

    def from_slot(k):
        source = (me + slots - k) % slots
        return pltpu.make_async_remote_copy(
            src_ref=tiles_ref.at[source], dst_ref=held.at[op, source],
            send_sem=send_slot.at[k], recv_sem=recv_slot.at[k],
            device_id=slot_device(source), device_id_type=mesh_ids,
        )

    def across(k, row, sends, receives, at, device):
        source = (me + slots - k) % slots
        return pltpu.make_async_remote_copy(
            src_ref=held.at[row, source], dst_ref=held.at[row, source],
            send_sem=sends.at[at], recv_sem=receives.at[at],
            device_id=device, device_id_type=mesh_ids,
        )

    for o in range(right_count):
        for a in range(left_count):
            if o + a > 0:
                to_slot(o + a * right_count).start()
    total[...] = jnp.zeros_like(total)
    own.wait()

    def contract(o):
        for a in range(left_count):
            k = o + a * right_count
            across(k, near, send_near, recv_near, k, near_device).wait_recv()
            across(k, diagonal, send_near, recv_near, slots + k, near_device).wait_recv()
        block = (ib + right_count - o) % right_count

        def one(j, carry):
            across_c = pl.ds(pl.multiple_of(j * lanes, lanes), lanes)
            left = amps_ref[
                :, across_c, pl.ds(pl.multiple_of(block * depth, lanes), depth)
            ].reshape(pairs * lanes, depth)
            right = jnp.concatenate(
                [
                    jnp.concatenate(
                        [
                            held[g, a * right_count + block, b * share : (b + 1) * share, across_c]
                            for g in range(4)
                        ],
                        axis=0,
                    )
                    for a in range(left_count)
                    for b in range(right_rows)
                ],
                axis=1,
            )
            total[...] += jnp.dot(left, right, preferred_element_type=jnp.float32)
            return carry

        lax.fori_loop(0, parts, one, 0)

    def step(o, carry):
        @pl.when(o < right_count)
        def _():
            for a in range(left_count):
                k = o + a * right_count

                @pl.when(k > 0)
                def _():
                    from_slot(k).wait_recv()

                across(k, op, send_far, recv_far, k, far_device).start()
                across(k, op, send_near, recv_near, k, near_device).start()
            for a in range(left_count):
                k = o + a * right_count
                across(k, far, send_far, recv_far, k, far_device).wait_recv()
                across(k, far, send_near, recv_near, slots + k, near_device).start()

        @pl.when(o == 0)
        def _():
            load.wait()

        @pl.when(o > 0)
        def _():
            contract(o - 1)

        return carry

    lax.fori_loop(0, right_count + 1, step, 0)

    row = lax.broadcasted_iota(jnp.int32, (lanes, columns), 0)
    column = lax.broadcasted_iota(jnp.int32, (lanes, columns), 1) % lanes
    for p in range(pairs):
        block = total[p * lanes : (p + 1) * lanes, :]
        part[p : p + 1, :] = jnp.sum(jnp.where(row == column, block, 0.0), axis=0, keepdims=True)

    def to_sum(k):
        return pltpu.make_async_remote_copy(
            src_ref=part, dst_ref=sums.at[k],
            send_sem=send_sum.at[k], recv_sem=recv_sum.at[k],
            device_id=slot_device((me + k) % slots), device_id_type=mesh_ids,
        )

    for k in range(1, slots):
        to_sum(k).start()
    for k in range(slots):
        if k > 0:
            to_slot(k).wait_send()
        across(k, op, send_far, recv_far, k, far_device).wait_send()
        across(k, op, send_near, recv_near, k, near_device).wait_send()
        across(k, far, send_near, recv_near, slots + k, near_device).wait_send()
    value = part[...]
    for k in range(1, slots):
        to_sum(k).wait_recv()
        value = value + sums[k]
    for k in range(1, slots):
        to_sum(k).wait_send()
    out_ref[...] = value


def spread_and_contract(tiles, amplitudes, right_rows):
    slots, rows, width = tiles.shape
    pairs, _, full = amplitudes.shape
    left_count, right_count = lax.axis_size("ia"), lax.axis_size("ib")
    columns = left_count * right_rows * lanes
    dma = pltpu.SemaphoreType.DMA
    return pl.pallas_call(
        functools.partial(spread_kernel, left_count, right_count, right_rows),
        out_shape=jax.ShapeDtypeStruct((pairs, columns), jnp.float32),
        in_specs=[pl.BlockSpec(memory_space=pltpu.VMEM), pl.BlockSpec(memory_space=pl.ANY)],
        out_specs=pl.BlockSpec(memory_space=pltpu.VMEM),
        scratch_shapes=[
            pltpu.VMEM((pairs, width, full), jnp.bfloat16),
            pltpu.VMEM((4, slots, rows, width), jnp.bfloat16),
            pltpu.VMEM((pairs * lanes, columns), jnp.float32),
            pltpu.VMEM((pairs, columns), jnp.float32),
            pltpu.VMEM((slots, pairs, columns), jnp.float32),
            dma, dma,
            dma((slots,)), dma((slots,)), dma((slots,)), dma((slots,)),
            dma((2 * slots,)), dma((2 * slots,)), dma((slots,)), dma((slots,)),
        ],
        compiler_params=pltpu.CompilerParams(
            collective_id=0, has_side_effects=True, vmem_limit_bytes=56 * 2**20
        ),
        cost_estimate=pl.CostEstimate(
            flops=2 * pairs * lanes * columns * full * (width // lanes),
            bytes_accessed=2 * (pairs * width * full + tiles.size),
            transcendentals=0,
        ),
    )(tiles, amplitudes)


def fused(fit_coefficients, three_center, amplitudes, slot_tiles):
    _, own_rows, aux = fit_coefficients.shape
    right_rows, _, share = three_center.shape
    local_pairs, tile_width, _ = amplitudes.shape
    slots = lax.axis_size("ia") * lax.axis_size("ib")
    center = jnp.transpose(three_center, (0, 2, 1)).reshape(right_rows * share, aux)
    gathered = lax.all_gather(fit_coefficients[0], ("ib", "op"), axis=0, tiled=True)
    tiles = integral_tiles(gathered.reshape(slots, tile_width, aux), center, slot_tiles)
    value = spread_and_contract(tiles, amplitudes, right_rows)
    return value.reshape(local_pairs, lax.axis_size("ia"), right_rows, lanes).sum(axis=3)


def whole_at_once(fit_coefficients, three_center, amplitudes, slot_tiles):
    left_rows = fit_coefficients.shape[0]
    right_rows = three_center.shape[0]
    share = three_center.shape[2]
    tile_width = amplitudes.shape[1]
    local_pairs = amplitudes.shape[0]
    left_count, right_count = lax.axis_size("ia"), lax.axis_size("ib")
    group_count = lax.axis_size("op")
    slot_count = left_count * right_count
    tiles = jnp.einsum(
        "oiu,tup->otip",
        lax.all_gather(fit_coefficients, ("ib", "op"), axis=1, tiled=True),
        three_center,
        preferred_element_type=jnp.float32,
    ).astype(jnp.bfloat16)
    tiles = tiles.reshape(left_rows, right_rows, slot_count, tile_width, share)
    ordered = jnp.concatenate(
        [lax.dynamic_slice_in_dim(tiles, slot_tiles[s], 1, axis=2) for s in range(slot_count)],
        axis=2,
    )
    arrived = lax.all_to_all(ordered, ("ia", "ib"), split_axis=2, concat_axis=0, tiled=True)
    received = arrived.reshape(left_count, right_count, left_rows, right_rows, tile_width, share)
    split_amps = amplitudes.reshape(local_pairs, tile_width, right_count, group_count * share)
    value = jnp.einsum(
        "pkie,aiobke->paob",
        split_amps,
        lax.all_gather(received, "op", axis=5, tiled=True),
        preferred_element_type=jnp.float32,
    )
    return value.reshape(local_pairs, left_count * left_rows, right_rows)


def per_device(
    fit_coefficients,
    three_center,
    amplitudes,
    pair_list,
    slot_tiles,
    energy_occupied,
    energy_left,
    energy_right,
):
    left_rows, own_rows, _ = fit_coefficients.shape
    right_rows, _, share = three_center.shape
    local_pairs, tile_width, _ = amplitudes.shape
    arguments = (fit_coefficients, three_center, amplitudes, slot_tiles)
    fits = (
        left_rows == 1
        and lax.axis_size("op") == 4
        and (lax.axis_size("ia") * lax.axis_size("ib")) % 2 == 0
        and tile_width % lanes == 0
        and (4 * share) % lanes == 0
        and share % 16 == 0
        and local_pairs % 8 == 0
    )
    if fits:
        summed = fused(*arguments)
    else:
        summed = lax.psum(whole_at_once(*arguments), ("ia", "ib"))
    owned = lax.dynamic_slice(
        summed,
        (0, lax.axis_index("ia") * left_rows, 0),
        (local_pairs, left_rows, right_rows),
    )
    occupied = energy_occupied.shape[0]
    column = lax.broadcasted_iota(jnp.int32, (local_pairs, occupied), 1)
    occupied_one = jnp.sum(
        jnp.where(pair_list[:, 0:1] == column, energy_occupied[None, :], 0.0), axis=1
    )
    occupied_two = jnp.sum(
        jnp.where(pair_list[:, 1:2] == column, energy_occupied[None, :], 0.0), axis=1
    )
    occupied_sum = occupied_one + occupied_two
    denominator = (
        energy_left[None, :, None] + energy_right[None, None, :] - occupied_sum[:, None, None]
    )
    factor = jnp.zeros_like(denominator)
    for point, weight in zip(laplace_points, laplace_weights):
        factor = factor + weight * jnp.exp(-point * denominator)
    return owned * factor


def solution(mesh):
    placed = (
        P("ia", ("ib", "op"), None),
        P(None, None, ("ib", "op")),
        P("op", ("ia", "ib"), None),
        P("op", None),
        P(),
        P(),
        P("ia"),
        P(),
    )
    return jax.shard_map(
        per_device, mesh=mesh, in_specs=placed, out_specs=P("op", "ia", None), check_vma=False
    )
```
